512 devices in a mesh: dp: 16 (over y_lo, x, core), seq: 32 (over y_hi, z).
Axes of the slice: x: 4, y: 8 (y_hi: 4, y_lo: 2; y = y_hi * 2 + y_lo), z: 8, core: 2. Of those that a mesh axis runs over, the one named last changes fastest.
Arguments:
- query_raw: bfloat16 [32, 16, 2048, 128], P('dp', None, 'seq'), may hold values from -6 to 6
- key_raw: bfloat16 [32, 16, 2048, 128], P('dp', None, 'seq'), may hold values from -6 to 6
- values: bfloat16 [32, 16, 2048, 128], P('dp', None, 'seq'), may hold values from -6 to 6
- residuals: bfloat16 [3, 32, 16, 2048, 128], P(None, 'dp', None, 'seq'), may hold values from -6 to 6
- block_section: int32 [3], replicated, may hold values from 0 to 31
- gain_query: float32 [128], replicated, may hold values from 0.5 to 2
- gain_key: float32 [128], replicated, may hold values from 0.5 to 2
Outputs:
- grad_query: bfloat16 [32, 16, 2048, 128], P('dp', None, 'seq')
- grad_key: bfloat16 [32, 16, 2048, 128], P('dp', None, 'seq')
- grad_values: bfloat16 [32, 16, 2048, 128], P('dp', None, 'seq')
- grad_gains: float32 [256], P('dp')
The draws below stay inside these ranges and needn't reach their ends.
Inputs may be any that keep to these rules, and one draw needn't show every extreme that they name: `block_section`: section indices.
All inputs are finite; a program needn't handle non-finite values.
Results may differ from the reference program's by a relative error of at most 0.012.
The reference program's roundings to bfloat16 on the way (of `grad_out` and `grad_scores`) count: a program that leaves them out, or rounds other values in their place, can miss the bound.
Values may be sent and summed in bfloat16 or wider, within the bound.
A program may use at most 64 MiB of HBM per device.

```python
import math
import jax
import jax.numpy as jnp
from jax import lax

HEADS = 16
HEAD_DIM = 128
TOK_LOCAL = 64
CTRL_BLOCKS = 3
LENGTH = 2048
LATENTS = 32
N_SEQ = 32


def levels(own_key, dims, shards, smallest, largest):
    level, own = 1.0, jax.random.fold_in(own_key, 6)
    for position, blocks in shards:
        heights = jnp.exp(jax.random.uniform(jax.random.fold_in(own, position), (blocks,), jnp.float32, smallest / len(shards), largest / len(shards)))
        level = level * jnp.repeat(heights, dims[position] // blocks).reshape([-1 if axis == position else 1 for axis in range(len(dims))])
    return level


def scatter_about(key, shape, width, reach, cuts=(), kind=jnp.bfloat16):
    values = width * jax.random.normal(key, shape, jnp.float32)
    if cuts:
        values = values * levels(key, shape, cuts, -0.22, 0.18)
    return jnp.clip(values, -reach, reach).astype(kind)


def setup_inputs(seed: int = 0) -> dict:
    keys = jax.random.split(jax.random.key(seed), 8)
    query_raw = scatter_about(keys[0], (LATENTS, HEADS, LENGTH, HEAD_DIM), 1.0, 6.0, ((0, 16), (2, 32)))
    key_raw = scatter_about(keys[1], (LATENTS, HEADS, LENGTH, HEAD_DIM), 1.0, 6.0, ((0, 16), (2, 32)))
    values = scatter_about(keys[2], (LATENTS, HEADS, LENGTH, HEAD_DIM), 1.0, 6.0, ((0, 16), (2, 32)))
    residuals = scatter_about(keys[3], (CTRL_BLOCKS, LATENTS, HEADS, LENGTH, HEAD_DIM), 1.0, 6.0, ((1, 16), (3, 32)))
    block_section = jax.random.randint(keys[4], (CTRL_BLOCKS,), 0, N_SEQ).astype(jnp.int32)
    gain_query = jnp.clip(jnp.exp(jax.random.uniform(keys[5], (HEAD_DIM,), jnp.float32, math.log(0.5), math.log(2.0))), 0.5, 2.0)
    gain_key = jnp.clip(jnp.exp(jax.random.uniform(keys[6], (HEAD_DIM,), jnp.float32, math.log(0.5), math.log(2.0))), 0.5, 2.0)
    return {"query_raw": query_raw, "key_raw": key_raw, "values": values, "residuals": residuals, "block_section": block_section, "gain_query": gain_query, "gain_key": gain_key}


epsilon = 1e-06

def normalize(tensor):
    entries = tensor.astype(jnp.float32)
    inverse = lax.rsqrt(lax.optimization_barrier(jnp.mean(entries * entries, axis=-1, keepdims=True)) + epsilon)
    return (entries * inverse, inverse)

def restore(unit, inverse, grad_norm, gain):
    grad_unit = grad_norm * gain
    return inverse * (grad_unit - unit * lax.optimization_barrier(jnp.mean(grad_unit * unit, axis=-1, keepdims=True)))

def one_item(operands, gain_query, gain_key):
    query, key, value, grad_out = operands
    score_scale = query.shape[-1] ** (-0.5)
    query_unit, query_inverse = normalize(query)
    key_unit, key_inverse = normalize(key)
    query_norm = (query_unit * gain_query).astype(jnp.bfloat16)
    key_norm = (key_unit * gain_key).astype(jnp.bfloat16)
    scores = jnp.dot(query_norm, key_norm.T, preferred_element_type=jnp.float32) * score_scale
    weights = jnp.exp(scores)
    probs = weights / lax.optimization_barrier(jnp.sum(weights, axis=-1, keepdims=True))
    grad_probs = jnp.dot(grad_out, value.T, preferred_element_type=jnp.float32)
    centre = lax.optimization_barrier(jnp.sum(probs * grad_probs, axis=-1, keepdims=True))
    grad_scores = (probs * (grad_probs - centre)).astype(jnp.bfloat16)
    grad_qnorm = jnp.dot(grad_scores, key_norm, preferred_element_type=jnp.float32) * score_scale
    grad_knorm = jnp.dot(grad_scores.T, query_norm, preferred_element_type=jnp.float32) * score_scale
    grad_value = jnp.dot(probs.astype(jnp.bfloat16).T, grad_out, preferred_element_type=jnp.float32)
    grad_q = restore(query_unit, query_inverse, grad_qnorm, gain_query).astype(jnp.bfloat16)
    grad_k = restore(key_unit, key_inverse, grad_knorm, gain_key).astype(jnp.bfloat16)
    part_query = lax.optimization_barrier(jnp.sum(grad_qnorm * query_unit, axis=0))
    part_key = lax.optimization_barrier(jnp.sum(grad_knorm * key_unit, axis=0))
    return (grad_q, grad_k, grad_value.astype(jnp.bfloat16), part_query, part_key)

def reference(query_raw, key_raw, values, residuals, block_section, gain_query, gain_key):
    positions = jnp.arange(LENGTH, dtype=jnp.int32)
    total = jnp.zeros(query_raw.shape, jnp.float32)
    for block_index in range(CTRL_BLOCKS):
        section = block_section[block_index].astype(jnp.int32)
        source = (positions % N_SEQ - section) % N_SEQ * TOK_LOCAL + positions // N_SEQ
        picked = jnp.take(residuals[block_index], source.astype(jnp.int32), axis=2)
        total = total + picked.astype(jnp.float32)
    grad_out = total.astype(jnp.bfloat16)
    item_total = LATENTS * HEADS
    operands = (query_raw.reshape(item_total, LENGTH, HEAD_DIM), key_raw.reshape(item_total, LENGTH, HEAD_DIM), values.reshape(item_total, LENGTH, HEAD_DIM), grad_out.reshape(item_total, LENGTH, HEAD_DIM))

    def apply_item(pieces):
        return one_item(pieces, gain_query, gain_key)
    grad_q, grad_k, grad_v, part_query, part_key = lax.map(apply_item, operands)
    full_shape = (LATENTS, HEADS, LENGTH, HEAD_DIM)
    grad_gains = jnp.concatenate([lax.optimization_barrier(jnp.sum(part_query, axis=0)), lax.optimization_barrier(jnp.sum(part_key, axis=0))])
    return (grad_q.reshape(full_shape), grad_k.reshape(full_shape), grad_v.reshape(full_shape), grad_gains)
```

```python
import functools
import math

import jax
import jax.numpy as jnp
from jax import lax
from jax.experimental import pallas as pl
from jax.experimental.pallas import tpu as pltpu
from jax.sharding import PartitionSpec as P

MESH = pl.DeviceIdType.MESH
epsilon = 1e-06
NY, NZ = 4, 8
QB = 256
KT = 512
BF, F32 = jnp.bfloat16, jnp.float32


def dot(a, b, dims):
    return lax.dot_general(a, b, (dims, ((), ())), preferred_element_type=F32)


def normalize(entries):
    inverse = lax.rsqrt(jnp.mean(entries * entries, axis=-1, keepdims=True) + epsilon)
    return entries * inverse, inverse


def restore(unit, inverse, grad_norm, gain):
    grad_unit = grad_norm * gain
    return inverse * (grad_unit - unit * jnp.mean(grad_unit * unit, axis=-1, keepdims=True))


def kernel(
    sec, gain_q, gain_k, q_in, k_in, v_in, r_in,
    q_out, k_out, v_out, g_out,
    k_mid, v_mid, q_mid, r_mid0, r_mid1, r_mid2, r_mid3,
    k_land, v_land, q_land, r_land0, r_land1, r_land2, r_land3,
    kn, knt, do_f, do_b, e_buf, dp_buf, dk_acc, dv_acc,
    dq_stage, dk_stage, dv_stage, dq_mid, dk_mid_a, dk_mid_b, dv_mid,
    g_part, g_z, g_y, g_d,
    sem1, sem2, send1, send2, gsem, gsend,
):
    me = lax.axis_index("seq")
    dp = lax.axis_index("dp")
    y, z = me // NZ, me % NZ
    scale = 128 ** (-0.5)
    r_mid = (r_mid0, r_mid1, r_mid2, r_mid3)
    r_land = (r_land0, r_land1, r_land2, r_land3)
    n_dp = g_d.shape[0]

    def at_z(dz):
        return {"seq": y * NZ + (z + dz) % NZ}

    def at_y(dy):
        return {"seq": ((y + dy) % NY) * NZ + z}

    barrier = pltpu.get_barrier_semaphore()
    for dz in range(1, NZ):
        pl.semaphore_signal(barrier, 1, device_id=at_z(dz), device_id_type=MESH)
    for dy in range(1, NY):
        pl.semaphore_signal(barrier, 1, device_id=at_y(dy), device_id_type=MESH)
    for dd in range(1, n_dp):
        pl.semaphore_signal(barrier, 1, device_id={"dp": (dp + dd) % n_dp}, device_id_type=MESH)
    pl.semaphore_wait(barrier, NZ - 1 + NY - 1 + n_dp - 1)

    def local(src, dst, sem):
        pltpu.make_async_copy(src, dst, sem).start()

    def remote(src, dst, send, recv, device):
        pltpu.make_async_remote_copy(
            src_ref=src, dst_ref=dst, send_sem=send, recv_sem=recv, device_id=device, device_id_type=MESH
        ).start()

    def wait(ref, sem):
        pltpu.make_async_copy(ref, ref, sem).wait()

    zo = (4, 3, 5, 2, 6, 1, 7)
    yo = (2, 1, 3)

    def first(n, path, src, mid):
        if path == "a":
            local(src.at[:, z], mid.at[z], sem1.at[n])
            for dz in zo:
                remote(src.at[:, (z + dz) % NZ], mid.at[z], send1.at[n], sem1.at[n], at_z(dz))
        else:
            local(src.at[y], mid.at[y], sem1.at[n])
            for dy in yo:
                remote(src.at[(y + dy) % NY], mid.at[y], send1.at[n], sem1.at[n], at_y(dy))

    def second(n, path, mid, land):
        wait(mid, sem1.at[n])
        if path == "a":
            local(mid.at[:, y], land.at[y], sem2.at[n])
            for dy in yo:
                remote(mid.at[:, (y + dy) % NY], land.at[y], send2.at[n], sem2.at[n], at_y(dy))
        else:
            local(mid.at[:, z], land.at[:, z], sem2.at[n])
            for dz in zo:
                remote(mid.at[:, (z + dz) % NZ], land.at[:, z], send2.at[n], sem2.at[n], at_z(dz))

    def sent(n, path, mid):
        if path == "a":
            wait(mid.at[pl.ds(0, NZ - 1)], send1.at[n])
            wait(mid.at[:, pl.ds(0, NY - 1)], send2.at[n])
        else:
            wait(mid.at[pl.ds(0, NY - 1)], send1.at[n])
            wait(mid.at[:, pl.ds(0, NZ - 1)], send2.at[n])

    low, high = pl.ds(0, 32), pl.ds(32, 32)
    streams = [
        ("a", k_in, k_mid, k_land),
        ("b", v_in, v_mid, v_land),
        ("a", q_in.at[:, :, low], q_mid.at[0].reshape(NZ, NY, 32, 128), q_land.at[:, :, low]),
        ("b", q_in.at[:, :, high], q_mid.at[1].reshape(NY, NZ, 32, 128), q_land.at[:, :, high]),
    ]
    for c in range(4):
        for i in range(3):
            path = ("a", "b", "ab"[c % 2])[i]
            shape = (NZ, NY, 16, 128) if path == "a" else (NY, NZ, 16, 128)
            streams.append(
                (path, r_in.at[i, :, :, pl.ds(16 * c, 16)], r_mid[c].at[i].reshape(*shape), r_land[c].at[i])
            )
    n_in = len(streams)

    for n, (path, src, mid, land) in enumerate(streams):
        first(n, path, src, mid)
    for n, (path, src, mid, land) in enumerate(streams):
        second(n, path, mid, land)

    wait(k_land, sem2.at[0])
    for t in range(NY):
        unit, _ = normalize(k_land[t].reshape(512, 128).astype(F32))
        norm = unit * gain_k[...]
        kn[pl.ds(512 * t, 512), :] = norm.astype(BF)
        knt[:, pl.ds(512 * t, 512)] = norm.T.astype(BF)
    dk_acc[...] = jnp.zeros_like(dk_acc)
    dv_acc[...] = jnp.zeros_like(dv_acc)
    wait(v_land, sem2.at[1])
    wait(q_land.at[:, :, low], sem2.at[2])
    wait(q_land.at[:, :, high], sem2.at[3])

    def queries(c, b, part_q):
        raw = q_land[c, pl.ds(4 * b, 4)].reshape(QB, 128).astype(F32)
        unit, inverse = normalize(raw)
        qn = (unit * gain_q[...]).astype(BF)
        go = do_b[pl.ds(pl.multiple_of(QB * b, QB), QB), :]

        def one(t, carry):
            total, mixed = carry
            keys = pl.ds(pl.multiple_of(KT * t, KT), KT)
            weights = jnp.exp2(dot(kn[keys, :], qn, ((1,), (1,))) * (scale * math.log2(math.e)))
            grad_probs = dot(v_land[t].reshape(KT, 128), go, ((1,), (1,)))
            e_buf[keys, :] = weights
            dp_buf[keys, :] = grad_probs
            return (
                total + jnp.sum(weights, axis=0, keepdims=True),
                mixed + jnp.sum(weights * grad_probs, axis=0, keepdims=True),
            )

        zero = jnp.zeros((1, QB), F32)
        total, mixed = lax.fori_loop(0, 2048 // KT, one, (zero, zero))
        over = 1.0 / total
        centre = mixed * over

        def two(t, dqt):
            keys = pl.ds(pl.multiple_of(KT * t, KT), KT)
            probs = e_buf[keys, :] * over
            grad_scores = (probs * (dp_buf[keys, :] - centre)).astype(BF)
            dk_acc[keys, :] += dot(grad_scores, qn, ((1,), (0,)))
            dv_acc[keys, :] += dot(probs.astype(BF), go, ((1,), (0,)))
            return dqt + dot(knt[:, keys], grad_scores, ((1,), (0,)))

        dqt = lax.fori_loop(0, 2048 // KT, two, jnp.zeros((128, QB), F32))
        grad_norm = dqt.T * scale
        out = restore(unit, inverse, grad_norm, gain_q[...]).astype(BF)
        dq_stage[c, pl.ds(4 * b, 4)] = out.reshape(4, 64, 128)
        return part_q + jnp.sum(grad_norm * unit, axis=0, keepdims=True)

    n_dq = n_in

    def send_dq(c):
        local(dq_stage.at[c, z], dq_mid.at[z, c], sem1.at[n_dq])
        for dz in zo:
            remote(
                dq_stage.at[c, (z + dz) % NZ], dq_mid.at[z, c], send1.at[n_dq], sem1.at[n_dq], at_z(dz)
            )

    part_q = jnp.zeros((1, 128), F32)
    for c in range(4):
        for i in range(3):
            wait(r_land[c].at[i], sem2.at[4 + 3 * c + i])
        if c == 3:
            for done in range(3):
                send_dq(done)
        for r in range(32):
            total = None
            for i in range(3):
                d = (r + 32 - sec[i]) % 32
                row = r_land[c][i, d // NZ, d % NZ].astype(F32)
                total = row if total is None else total + row
            do_f[:, r, :] = total
        do_b[...] = do_f[...].reshape(512, 128).astype(BF)
        part_q = lax.fori_loop(0, 2, lambda b, p, c=c: queries(c, b, p), part_q)
    send_dq(3)

    for t in range(NY):
        dv_stage[t] = dv_acc[pl.ds(512 * t, 512), :].astype(BF).reshape(NZ, 64, 128)
    n_dv, n_dka, n_dkb = n_in + 1, n_in + 2, n_in + 3
    first(n_dv, "b", dv_stage, dv_mid)
    part_k = jnp.zeros((1, 128), F32)
    for t in range(NY):
        unit, inverse = normalize(k_land[t].reshape(512, 128).astype(F32))
        grad_norm = dk_acc[pl.ds(512 * t, 512), :] * scale
        part_k = part_k + jnp.sum(grad_norm * unit, axis=0, keepdims=True)
        out = restore(unit, inverse, grad_norm, gain_k[...]).astype(BF)
        dk_stage[t] = out.reshape(NZ, 64, 128)

    g_part[0, :, :] = jnp.concatenate([part_q, part_k, jnp.zeros((6, 128), F32)], axis=0)
    local(g_part.at[0], g_z.at[z], gsem.at[0])
    for dz in zo:
        remote(g_part.at[0], g_z.at[z], gsend.at[0], gsem.at[0], at_z(dz))

    first(n_dka, "a", dk_stage.at[:, :, low], dk_mid_a)
    first(n_dkb, "b", dk_stage.at[:, :, high], dk_mid_b)

    wait(g_z, gsem.at[0])
    g_part[1, :, :] = jnp.sum(g_z[...], axis=0)
    local(g_part.at[1], g_y.at[y], gsem.at[1])
    for dy in yo:
        remote(g_part.at[1], g_y.at[y], gsend.at[1], gsem.at[1], at_y(dy))

    second(n_dq, "a", dq_mid, q_out)

    wait(g_y, gsem.at[1])
    g_part[2, :, :] = jnp.sum(g_y[...], axis=0)
    local(g_part.at[2], g_d.at[dp], gsem.at[2])
    for dd in range(1, n_dp):
        remote(g_part.at[2], g_d.at[dp], gsend.at[2], gsem.at[2], {"dp": (dp + dd) % n_dp})

    second(n_dv, "b", dv_mid, v_out)
    second(n_dka, "a", dk_mid_a, k_out.at[:, :, low])
    second(n_dkb, "b", dk_mid_b, k_out.at[:, :, high])

    wait(g_d, gsem.at[2])
    g_out[...] = jnp.sum(g_d[...], axis=0)

    for n, (path, src, mid, land) in enumerate(streams):
        sent(n, path, mid)
    sent(n_dq, "a", dq_mid)
    sent(n_dv, "b", dv_mid)
    sent(n_dka, "a", dk_mid_a)
    sent(n_dkb, "b", dk_mid_b)
    wait(g_z.at[pl.ds(0, NZ - 1)], gsend.at[0])
    wait(g_y.at[pl.ds(0, NY - 1)], gsend.at[1])
    wait(g_d.at[pl.ds(0, n_dp - 1)], gsend.at[2])
    wait(q_out, sem2.at[n_dq])
    wait(v_out, sem2.at[n_dv])
    wait(k_out.at[:, :, low], sem2.at[n_dka])
    wait(k_out.at[:, :, high], sem2.at[n_dkb])


def on_device(query_raw, key_raw, values, residuals, block_section, gain_query, gain_key):
    n_dp = lax.axis_size("dp")
    local_shape = query_raw.shape
    grid = (NY, NZ, 64, 128)
    vmem, dma = pltpu.VMEM, pltpu.SemaphoreType.DMA
    block = functools.partial(vmem, dtype=BF)
    full = jax.ShapeDtypeStruct(grid, BF)
    scratch = [
        vmem((NZ, NY, 64, 128), BF), vmem(grid, BF), vmem((2, 32, 32, 128), BF),
        *[vmem((3, 32, 16, 128), BF)] * 4,
        vmem(grid, BF), vmem(grid, BF), vmem(grid, BF),
        *[vmem((3, NY, NZ, 16, 128), BF)] * 4,
        vmem((2048, 128), BF), vmem((128, 2048), BF),
        vmem((16, 32, 128), F32), vmem((512, 128), BF),
        vmem((2048, QB), F32), vmem((2048, QB), F32),
        vmem((2048, 128), F32), vmem((2048, 128), F32),
        vmem(grid, BF), vmem(grid, BF), vmem(grid, BF),
        vmem((NZ, NY, 64, 128), BF), vmem((NZ, NY, 32, 128), BF), vmem((NY, NZ, 32, 128), BF), vmem(grid, BF),
        vmem((3, 8, 128), F32), vmem((NZ, 8, 128), F32), vmem((NY, 8, 128), F32), vmem((n_dp, 8, 128), F32),
        dma((20,)), dma((20,)), dma((20,)), dma((20,)), dma((3,)), dma((3,)),
    ]
    anywhere = pl.BlockSpec(memory_space=pl.ANY)
    inside = pl.BlockSpec(memory_space=pltpu.VMEM)
    grad_q, grad_k, grad_v, gains = pl.pallas_call(
        kernel,
        out_shape=(full, full, full, jax.ShapeDtypeStruct((8, 128), F32)),
        in_specs=[pl.BlockSpec(memory_space=pltpu.SMEM), inside, inside] + [anywhere] * 4,
        out_specs=(anywhere, anywhere, anywhere, inside),
        scratch_shapes=scratch,
        compiler_params=pltpu.CompilerParams(
            collective_id=0, has_side_effects=True, vmem_limit_bytes=48 << 20
        ),
        name="attention_backward",
    )(
        block_section,
        gain_query.reshape(1, 128),
        gain_key.reshape(1, 128),
        query_raw.reshape(grid),
        key_raw.reshape(grid),
        values.reshape(grid),
        residuals.reshape((3,) + grid),
    )
    share = 256 // n_dp
    grad_gains = lax.dynamic_slice(gains.reshape(-1), (lax.axis_index("dp") * share,), (share,))
    return (
        grad_q.reshape(local_shape),
        grad_k.reshape(local_shape),
        grad_v.reshape(local_shape),
        grad_gains,
    )


def solution(mesh):
    placed = (
        P("dp", None, "seq", None),
        P("dp", None, "seq", None),
        P("dp", None, "seq", None),
        P(None, "dp", None, "seq", None),
        P(),
        P(),
        P(),
    )
    return jax.shard_map(
        on_device,
        mesh=mesh,
        in_specs=placed,
        out_specs=(
            P("dp", None, "seq", None),
            P("dp", None, "seq", None),
            P("dp", None, "seq", None),
            P("dp"),
        ),
        check_vma=False,
    )
```

```python
import math

import jax
import jax.numpy as jnp
from jax import lax
from jax.experimental import pallas as pl
from jax.experimental.pallas import tpu as pltpu
from jax.sharding import PartitionSpec as P

MESH = pl.DeviceIdType.MESH
epsilon = 1e-06
NY, NZ = 4, 8
QB = 512
BF, F32 = jnp.bfloat16, jnp.float32


def dot(a, b, dims):
    return lax.dot_general(a, b, (dims, ((), ())), preferred_element_type=F32)


def normalize(entries):
    inverse = lax.rsqrt(jnp.mean(entries * entries, axis=-1, keepdims=True) + epsilon)
    return entries * inverse, inverse


def restore(unit, inverse, grad_norm, gain):
    grad_unit = grad_norm * gain
    return inverse * (grad_unit - unit * jnp.mean(grad_unit * unit, axis=-1, keepdims=True))


def kernel(
    sec_in, gain_q_in, gain_k_in, q_in, k_in, v_in, r_in,
    q_out, k_out, v_out, g_out,
    k_mid, v_mid, q_mid, r_mid0, r_mid1, r_mid2, r_mid3,
    k_land, v_land, q_land, r_land0, r_land1, r_land2, r_land3,
    kn, qn, do_f, probs, probs_b, mixed, dk_acc, dv_acc,
    dq_stage, dk_stage, dv_stage, dq_mid_a, dq_mid_b, dk_mid_a, dk_mid_b, dv_mid,
    g_part, g_z, g_y, g_d, sec, gain_q, gain_k,
    sem1, sem2, send1, send2, gsem, gsend, own,
):
    me = lax.axis_index("seq")
    dp = lax.axis_index("dp")
    y, z = me // NZ, me % NZ
    scale = 128 ** (-0.5)
    r_mid = (r_mid0, r_mid1, r_mid2, r_mid3)
    r_land = (r_land0, r_land1, r_land2, r_land3)
    n_dp = g_d.shape[0]

    def at_z(dz):
        return {"seq": y * NZ + (z + dz) % NZ}

    def at_y(dy):
        return {"seq": ((y + dy) % NY) * NZ + z}

    barrier = pltpu.get_barrier_semaphore()
    for dz in range(1, NZ):
        pl.semaphore_signal(barrier, 1, device_id=at_z(dz), device_id_type=MESH)
    for dy in range(1, NY):
        pl.semaphore_signal(barrier, 1, device_id=at_y(dy), device_id_type=MESH)
    for dd in range(1, n_dp):
        pl.semaphore_signal(barrier, 1, device_id={"dp": (dp + dd) % n_dp}, device_id_type=MESH)
    pl.semaphore_wait(barrier, NZ - 1 + NY - 1 + n_dp - 1)

    def local(src, dst, sem):
        pltpu.make_async_copy(src, dst, sem).start()

    def remote(src, dst, send, recv, device):
        pltpu.make_async_remote_copy(
            src_ref=src, dst_ref=dst, send_sem=send, recv_sem=recv, device_id=device, device_id_type=MESH
        ).start()

    def wait(ref, sem):
        pltpu.make_async_copy(ref, ref, sem).wait()

    zo = (4, 3, 5, 2, 6, 1, 7)
    yo = (2, 1, 3)

    def first(n, path, src, mid):
        if path == "a":
            local(src.at[:, z], mid.at[z], sem1.at[n])
            for dz in zo:
                remote(src.at[:, (z + dz) % NZ], mid.at[z], send1.at[n], sem1.at[n], at_z(dz))
        else:
            local(src.at[y], mid.at[y], sem1.at[n])
            for dy in yo:
                remote(src.at[(y + dy) % NY], mid.at[y], send1.at[n], sem1.at[n], at_y(dy))

    def second(n, path, mid, land):
        wait(mid, sem1.at[n])
        if path == "a":
            local(mid.at[:, y], land.at[y], sem2.at[n])
            for dy in yo:
                remote(mid.at[:, (y + dy) % NY], land.at[y], send2.at[n], sem2.at[n], at_y(dy))
        else:
            local(mid.at[:, z], land.at[:, z], sem2.at[n])
            for dz in zo:
                remote(mid.at[:, (z + dz) % NZ], land.at[:, z], send2.at[n], sem2.at[n], at_z(dz))

    def sent(n, path, mid):
        if path == "a":
            wait(mid.at[pl.ds(0, NZ - 1)], send1.at[n])
            wait(mid.at[:, pl.ds(0, NY - 1)], send2.at[n])
        else:
            wait(mid.at[pl.ds(0, NY - 1)], send1.at[n])
            wait(mid.at[:, pl.ds(0, NZ - 1)], send2.at[n])

    low, high = pl.ds(0, 32), pl.ds(32, 32)
    streams = [
        ("a", k_in, k_mid, k_land),
        ("b", v_in, v_mid, v_land),
        ("a", q_in.at[:, :, low], q_mid.at[0].reshape(NZ, NY, 32, 128), q_land.at[:, :, low]),
        ("b", q_in.at[:, :, high], q_mid.at[1].reshape(NY, NZ, 32, 128), q_land.at[:, :, high]),
    ]
    for c in range(4):
        for i in range(3):
            path = ("a", "b", "ab"[c % 2])[i]
            shape = (NZ, NY, 16, 128) if path == "a" else (NY, NZ, 16, 128)
            streams.append(
                (path, r_in.at[i, :, :, pl.ds(16 * c, 16)], r_mid[c].at[i].reshape(*shape), r_land[c].at[i])
            )
    n_in = len(streams)

    for n, (path, src, mid, land) in enumerate(streams):
        first(n, path, src, mid)
    small = ((sec_in, sec), (gain_q_in, gain_q), (gain_k_in, gain_k))
    for n, (src, dst) in enumerate(small):
        local(src, dst, own.at[n])
    for n, (path, src, mid, land) in enumerate(streams):
        second(n, path, mid, land)
    for n, (src, dst) in enumerate(small):
        pltpu.make_async_copy(src, dst, own.at[n]).wait()

    wait(k_land, sem2.at[0])
    for t in range(NY):
        unit, _ = normalize(k_land[t].reshape(512, 128).astype(F32))
        kn[pl.ds(512 * t, 512), :] = (unit * gain_k[...]).astype(BF)
    dk_acc[...] = jnp.zeros_like(dk_acc)
    dv_acc[...] = jnp.zeros_like(dv_acc)
    wait(v_land, sem2.at[1])
    wait(q_land.at[:, :, low], sem2.at[2])
    wait(q_land.at[:, :, high], sem2.at[3])

    def before(c, carry):
        unit, _ = normalize(q_land[c].reshape(QB, 128).astype(F32))
        norm = (unit * gain_q[...]).astype(BF)
        qn[c] = norm
        weights = jnp.exp2(dot(kn[...], norm, ((1,), (1,))) * (scale * math.log2(math.e)))
        probs[c] = weights
        over = 1.0 / jnp.sum(weights, axis=0, keepdims=True)
        share = probs[c] * over
        upper = share.astype(BF)
        lower = (share - upper.astype(F32)).astype(BF)
        probs[c] = share
        probs_b[c] = upper
        held = v_land[...].reshape(2048, 128)
        mixed[c] = dot(held, upper, ((0,), (0,))) + dot(held, lower, ((0,), (0,)))
        return carry

    lax.fori_loop(0, 4, before, 0)

    n_dqa, n_dqb, n_dv, n_dka, n_dkb = range(n_in, n_in + 5)

    def send_dq(c):
        local(dq_stage.at[c, z, low], dq_mid_a.at[z, c], sem1.at[n_dqa])
        for dz in zo:
            remote(
                dq_stage.at[c, (z + dz) % NZ, low], dq_mid_a.at[z, c],
                send1.at[n_dqa], sem1.at[n_dqa], at_z(dz),
            )

        @pl.when(y == c)
        def _():
            local(dq_stage.at[c, :, high], dq_mid_b.at[y], sem1.at[n_dqb])

        @pl.when(y != c)
        def _():
            remote(
                dq_stage.at[c, :, high], dq_mid_b.at[y],
                send1.at[n_dqb], sem1.at[n_dqb], {"seq": c * NZ + z},
            )

    def after(c, part_q):
        for cc in range(4):

            @pl.when(c == cc)
            def _():
                for i in range(3):
                    wait(r_land[cc].at[i], sem2.at[4 + 3 * cc + i])
                if cc == 3:
                    for done in range(3):
                        send_dq(done)
                for r in range(32):
                    total = None
                    for i in range(3):
                        d = (r + 32 - sec[i]) % 32
                        row = r_land[cc][i, d // NZ, d % NZ].astype(F32)
                        total = row if total is None else total + row
                    do_f[pl.ds(r, 16, stride=32), :] = total

        grad_out = do_f[...].astype(BF)
        centre = jnp.sum(grad_out.astype(F32).T * mixed[c], axis=0, keepdims=True)
        grad_probs = dot(v_land[...].reshape(2048, 128), grad_out, ((1,), (1,)))
        grad_scores = (probs[c] * (grad_probs - centre)).astype(BF)
        dk_acc[...] += dot(grad_scores, qn[c], ((1,), (0,)))
        dv_acc[...] += dot(probs_b[c], grad_out, ((1,), (0,)))
        grad_norm = dot(kn[...], grad_scores, ((0,), (0,))).T * scale
        unit, inverse = normalize(q_land[c].reshape(QB, 128).astype(F32))
        out = restore(unit, inverse, grad_norm, gain_q[...]).astype(BF)
        dq_stage[c] = out.reshape(NZ, 64, 128)
        return part_q + jnp.sum(grad_norm * unit, axis=0, keepdims=True)

    part_q = lax.fori_loop(0, 4, after, jnp.zeros((1, 128), F32))
    send_dq(3)

    for t in range(NY):
        dv_stage[t] = dv_acc[pl.ds(512 * t, 512), :].astype(BF).reshape(NZ, 64, 128)
    first(n_dv, "b", dv_stage, dv_mid)
    part_k = jnp.zeros((1, 128), F32)
    for t in range(NY):
        unit, inverse = normalize(k_land[t].reshape(512, 128).astype(F32))
        grad_norm = dk_acc[pl.ds(512 * t, 512), :] * scale
        part_k = part_k + jnp.sum(grad_norm * unit, axis=0, keepdims=True)
        out = restore(unit, inverse, grad_norm, gain_k[...]).astype(BF)
        dk_stage[t] = out.reshape(NZ, 64, 128)

    g_part[0, :, :] = jnp.concatenate([part_q, part_k, jnp.zeros((6, 128), F32)], axis=0)
    local(g_part.at[0], g_z.at[z], gsem.at[0])
    for dz in zo:
        remote(g_part.at[0], g_z.at[z], gsend.at[0], gsem.at[0], at_z(dz))

    first(n_dka, "a", dk_stage.at[:, :, low], dk_mid_a)
    first(n_dkb, "b", dk_stage.at[:, :, high], dk_mid_b)

    wait(g_z, gsem.at[0])
    g_part[1, :, :] = jnp.sum(g_z[...], axis=0)
    local(g_part.at[1], g_y.at[y], gsem.at[1])
    for dy in yo:
        remote(g_part.at[1], g_y.at[y], gsend.at[1], gsem.at[1], at_y(dy))

    second(n_dqa, "a", dq_mid_a, q_out.at[:, :, low])
    second(n_dqb, "b", dq_mid_b, q_out.at[:, :, high])

    wait(g_y, gsem.at[1])
    g_part[2, :, :] = jnp.sum(g_y[...], axis=0)
    local(g_part.at[2], g_d.at[dp], gsem.at[2])
    for dd in range(1, n_dp):
        remote(g_part.at[2], g_d.at[dp], gsend.at[2], gsem.at[2], {"dp": (dp + dd) % n_dp})

    second(n_dv, "b", dv_mid, v_out)
    second(n_dka, "a", dk_mid_a, k_out.at[:, :, low])
    second(n_dkb, "b", dk_mid_b, k_out.at[:, :, high])

    wait(g_d, gsem.at[2])
    sums = jnp.sum(g_d[...], axis=0)
    per_row = 128 * n_dp // 256
    row = jnp.where(dp // per_row == 0, sums[0:1], sums[1:2])
    start = (dp % per_row) * (256 // n_dp)
    g_out[...] = pltpu.roll(jnp.broadcast_to(row, (8, 128)), (128 - start) % 128, 1)

    for n, (path, src, mid, land) in enumerate(streams):
        sent(n, path, mid)
    sent(n_dqa, "a", dq_mid_a)
    sent(n_dqb, "b", dq_mid_b)
    sent(n_dv, "b", dv_mid)
    sent(n_dka, "a", dk_mid_a)
    sent(n_dkb, "b", dk_mid_b)
    wait(g_z.at[pl.ds(0, NZ - 1)], gsend.at[0])
    wait(g_y.at[pl.ds(0, NY - 1)], gsend.at[1])
    wait(g_d.at[pl.ds(0, n_dp - 1)], gsend.at[2])
    wait(q_out.at[:, :, low], sem2.at[n_dqa])
    wait(q_out.at[:, :, high], sem2.at[n_dqb])
    wait(v_out, sem2.at[n_dv])
    wait(k_out.at[:, :, low], sem2.at[n_dka])
    wait(k_out.at[:, :, high], sem2.at[n_dkb])


def deliver(q_done, k_done, v_done, g_done, q_out, k_out, v_out, g_out, sem):
    pairs = ((q_done, q_out), (k_done, k_out), (v_done, v_out))
    copies = [
        pltpu.make_async_copy(src.at[part], dst.at[part], sem.at[n, part])
        for n, (src, dst) in enumerate(pairs)
        for part in range(NY)
    ]
    for copy in copies:
        copy.start()
    g_out[...] = g_done[0, 0 : g_out.shape[0]]
    for copy in copies:
        copy.wait()


def on_device(query_raw, key_raw, values, residuals, block_section, gain_query, gain_key):
    n_dp = lax.axis_size("dp")
    local_shape = query_raw.shape
    grid = (NY, NZ, 64, 128)
    vmem, dma = pltpu.VMEM, pltpu.SemaphoreType.DMA
    scratch = [
        vmem((NZ, NY, 64, 128), BF), vmem(grid, BF), vmem((2, 32, 32, 128), BF),
        *[vmem((3, 32, 16, 128), BF)] * 4,
        vmem(grid, BF), vmem(grid, BF), vmem(grid, BF),
        *[vmem((3, NY, NZ, 16, 128), BF)] * 4,
        vmem((2048, 128), BF), vmem((4, QB, 128), BF), vmem((QB, 128), F32),
        vmem((4, 2048, QB), F32), vmem((4, 2048, QB), BF), vmem((4, 128, QB), F32),
        vmem((2048, 128), F32), vmem((2048, 128), F32),
        vmem(grid, BF), vmem(grid, BF), vmem(grid, BF),
        *[vmem((NZ, NY, 32, 128), BF), vmem((NY, NZ, 32, 128), BF)] * 2, vmem(grid, BF),
        vmem((3, 8, 128), F32), vmem((NZ, 8, 128), F32), vmem((NY, 8, 128), F32), vmem((n_dp, 8, 128), F32),
        pltpu.SMEM((3,), jnp.int32), vmem((1, 128), F32), vmem((1, 128), F32),
        dma((21,)), dma((21,)), dma((21,)), dma((21,)), dma((3,)), dma((3,)), dma((3,)),
    ]
    anywhere = pl.BlockSpec(memory_space=pl.ANY)
    inside = pl.BlockSpec(memory_space=pltpu.VMEM)
    kept = pltpu.VMEM(grid, BF)
    operands = (
        block_section,
        gain_query.reshape(1, 128),
        gain_key.reshape(1, 128),
        query_raw.reshape(grid),
        key_raw.reshape(grid),
        values.reshape(grid),
        residuals.reshape((3,) + grid),
    )
    done = pl.pallas_call(
        kernel,
        out_shape=(kept, kept, kept, pltpu.VMEM((8, 128), F32)),
        in_specs=[anywhere] * 7,
        out_specs=(anywhere, anywhere, anywhere, inside),
        scratch_shapes=scratch,
        compiler_params=pltpu.CompilerParams(
            collective_id=0, has_side_effects=True, vmem_limit_bytes=56 << 20
        ),
        name="attention_backward",
    )(*[pltpu.with_memory_space_constraint(operand, pltpu.HBM) for operand in operands])
    full = jax.ShapeDtypeStruct(grid, BF)
    grad_q, grad_k, grad_v, grad_gains = pl.pallas_call(
        deliver,
        out_shape=(full, full, full, jax.ShapeDtypeStruct((256 // n_dp,), F32)),
        in_specs=[anywhere] * 3 + [inside],
        out_specs=(anywhere, anywhere, anywhere, inside),
        scratch_shapes=[dma((3, NY))],
        compiler_params=pltpu.CompilerParams(vmem_limit_bytes=1 << 20),
        name="deliver",
    )(*done)
    return (
        grad_q.reshape(local_shape),
        grad_k.reshape(local_shape),
        grad_v.reshape(local_shape),
        grad_gains,
    )


def solution(mesh):
    placed = (
        P("dp", None, "seq", None),
        P("dp", None, "seq", None),
        P("dp", None, "seq", None),
        P(None, "dp", None, "seq", None),
        P(),
        P(),
        P(),
    )
    return jax.shard_map(
        on_device,
        mesh=mesh,
        in_specs=placed,
        out_specs=(
            P("dp", None, "seq", None),
            P("dp", None, "seq", None),
            P("dp", None, "seq", None),
            P("dp"),
        ),
        check_vma=False,
    )
```

```python
import math

import jax
import jax.numpy as jnp
from jax import lax
from jax.experimental import pallas as pl
from jax.experimental.pallas import tpu as pltpu
from jax.sharding import PartitionSpec as P

MESH = pl.DeviceIdType.MESH
epsilon = 1e-06
NY, NZ = 4, 8
QB = 512
BF, F32 = jnp.bfloat16, jnp.float32


def dot(a, b, dims):
    return lax.dot_general(a, b, (dims, ((), ())), preferred_element_type=F32)


def normalize(entries):
    inverse = lax.rsqrt(jnp.mean(entries * entries, axis=-1, keepdims=True) + epsilon)
    return entries * inverse, inverse


def restore(unit, inverse, grad_norm, gain):
    grad_unit = grad_norm * gain
    return inverse * (grad_unit - unit * jnp.mean(grad_unit * unit, axis=-1, keepdims=True))


def kernel(
    sec_in, gain_q_in, gain_k_in, q_in, k_in, v_in, r_in,
    q_out, k_out, v_out, g_out,
    k_mid, v_mid, q_mid, r_mid0, r_mid1, r_mid2, r_mid3,
    k_land, v_land, q_land, r_land0, r_land1, r_land2, r_land3,
    kn, qn, do_f, probs, probs_b, mixed, dk_acc, dv_acc,
    dq_stage, dk_stage, dv_stage, dq_mid_a, dq_mid_b, dk_mid_a, dk_mid_b, dv_mid_a, dv_mid_b,
    g_part, g_z, g_y, g_d, sec, gain_q, gain_k,
    sem1, sem2, send1, send2, gsem, gsend, own,
):
    me = lax.axis_index("seq")
    dp = lax.axis_index("dp")
    y, z = me // NZ, me % NZ
    scale = 128 ** (-0.5)
    r_mid = (r_mid0, r_mid1, r_mid2, r_mid3)
    r_land = (r_land0, r_land1, r_land2, r_land3)
    n_dp = g_d.shape[0]

    def at_z(dz):
        return {"seq": y * NZ + (z + dz) % NZ}

    def at_y(dy):
        return {"seq": ((y + dy) % NY) * NZ + z}

    barrier = pltpu.get_barrier_semaphore()
    for dz in range(1, NZ):
        pl.semaphore_signal(barrier, 1, device_id=at_z(dz), device_id_type=MESH)
    for dy in range(1, NY):
        pl.semaphore_signal(barrier, 1, device_id=at_y(dy), device_id_type=MESH)
    for dd in range(1, n_dp):
        pl.semaphore_signal(barrier, 1, device_id={"dp": (dp + dd) % n_dp}, device_id_type=MESH)
    def local(src, dst, sem):
        pltpu.make_async_copy(src, dst, sem).start()

    def remote(src, dst, send, recv, device):
        pltpu.make_async_remote_copy(
            src_ref=src, dst_ref=dst, send_sem=send, recv_sem=recv, device_id=device, device_id_type=MESH
        ).start()

    def wait(ref, sem):
        pltpu.make_async_copy(ref, ref, sem).wait()

    zo = (4, 3, 5, 2, 6, 1, 7)
    yo = (2, 1, 3)

    def keep(n, path, src, mid):
        if path == "a":
            local(src.at[:, z], mid.at[z], sem1.at[n])
        else:
            local(src.at[y], mid.at[y], sem1.at[n])

    def first(n, path, src, mid):
        if path == "a":
            for dz in zo:
                remote(src.at[:, (z + dz) % NZ], mid.at[z], send1.at[n], sem1.at[n], at_z(dz))
        else:
            for dy in yo:
                remote(src.at[(y + dy) % NY], mid.at[y], send1.at[n], sem1.at[n], at_y(dy))

    def second(n, path, mid, land):
        wait(mid, sem1.at[n])
        if path == "a":
            local(mid.at[:, y], land.at[y], sem2.at[n])
            for dy in yo:
                remote(mid.at[:, (y + dy) % NY], land.at[y], send2.at[n], sem2.at[n], at_y(dy))
        else:
            local(mid.at[:, z], land.at[:, z], sem2.at[n])
            for dz in zo:
                remote(mid.at[:, (z + dz) % NZ], land.at[:, z], send2.at[n], sem2.at[n], at_z(dz))

    def sent(n, path, mid):
        if path == "a":
            wait(mid.at[pl.ds(0, NZ - 1)], send1.at[n])
            wait(mid.at[:, pl.ds(0, NY - 1)], send2.at[n])
        else:
            wait(mid.at[pl.ds(0, NY - 1)], send1.at[n])
            wait(mid.at[:, pl.ds(0, NZ - 1)], send2.at[n])

    low, high = pl.ds(0, 32), pl.ds(32, 32)
    streams = [
        ("a", k_in, k_mid, k_land),
        ("b", v_in, v_mid, v_land),
        ("a", q_in.at[:, :, low], q_mid.at[0].reshape(NZ, NY, 32, 128), q_land.at[:, :, low]),
        ("b", q_in.at[:, :, high], q_mid.at[1].reshape(NY, NZ, 32, 128), q_land.at[:, :, high]),
    ]
    for c in range(4):
        for i in range(3):
            path = ("a", "b", "ab"[c % 2])[i]
            shape = (NZ, NY, 16, 128) if path == "a" else (NY, NZ, 16, 128)
            streams.append(
                (path, r_in.at[i, :, :, pl.ds(16 * c, 16)], r_mid[c].at[i].reshape(*shape), r_land[c].at[i])
            )
    n_in = len(streams)

    small = ((sec_in, sec), (gain_q_in, gain_q), (gain_k_in, gain_k))
    for n, (src, dst) in enumerate(small):
        local(src, dst, own.at[n])
    for n, (path, src, mid, land) in enumerate(streams):
        keep(n, path, src, mid)
    pl.semaphore_wait(barrier, NZ - 1 + NY - 1 + n_dp - 1)
    for n, (path, src, mid, land) in enumerate(streams):
        first(n, path, src, mid)
    for n, (path, src, mid, land) in enumerate(streams):
        second(n, path, mid, land)
    for n, (src, dst) in enumerate(small):
        pltpu.make_async_copy(src, dst, own.at[n]).wait()

    wait(k_land, sem2.at[0])
    for t in range(NY):
        unit, _ = normalize(k_land[t].reshape(512, 128).astype(F32))
        kn[pl.ds(512 * t, 512), :] = (unit * gain_k[...]).astype(BF)
    dk_acc[...] = jnp.zeros_like(dk_acc)
    dv_acc[...] = jnp.zeros_like(dv_acc)
    wait(v_land, sem2.at[1])
    wait(q_land.at[:, :, low], sem2.at[2])
    wait(q_land.at[:, :, high], sem2.at[3])

    def before(c, carry):
        unit, _ = normalize(q_land[c].reshape(QB, 128).astype(F32))
        norm = (unit * gain_q[...]).astype(BF)
        qn[c] = norm
        weights = jnp.exp2(dot(kn[...], norm, ((1,), (1,))) * (scale * math.log2(math.e)))
        probs[c] = weights
        over = 1.0 / jnp.sum(weights, axis=0, keepdims=True)
        share = probs[c] * over
        upper = share.astype(BF)
        lower = (share - upper.astype(F32)).astype(BF)
        probs[c] = share
        probs_b[c] = upper
        held = v_land[...].reshape(2048, 128)
        mixed[c] = dot(held, upper, ((0,), (0,))) + dot(held, lower, ((0,), (0,)))
        return carry

    lax.fori_loop(0, 4, before, 0)

    n_dqa, n_dqb, n_dva, n_dvb, n_dka, n_dkb = range(n_in, n_in + 6)
    g_part[...] = jnp.zeros_like(g_part)

    def send_dq(c):
        local(dq_stage.at[c, z, low], dq_mid_a.at[z, c], sem1.at[n_dqa])
        for dz in zo:
            remote(
                dq_stage.at[c, (z + dz) % NZ, low], dq_mid_a.at[z, c],
                send1.at[n_dqa], sem1.at[n_dqa], at_z(dz),
            )

        @pl.when(y == c)
        def _():
            local(dq_stage.at[c, :, high], dq_mid_b.at[y], sem1.at[n_dqb])

        @pl.when(y != c)
        def _():
            remote(
                dq_stage.at[c, :, high], dq_mid_b.at[y],
                send1.at[n_dqb], sem1.at[n_dqb], {"seq": c * NZ + z},
            )

    def after(c, part_q):
        for cc in range(4):

            @pl.when(c == cc)
            def _():
                for i in range(3):
                    wait(r_land[cc].at[i], sem2.at[4 + 3 * cc + i])
                for r in range(32):
                    total = None
                    for i in range(3):
                        d = (r + 32 - sec[i]) % 32
                        row = r_land[cc][i, d // NZ, d % NZ].astype(F32)
                        total = row if total is None else total + row
                    do_f[pl.ds(r, 16, stride=32), :] = total

        grad_out = do_f[...].astype(BF)
        dv_acc[...] += dot(probs_b[c], grad_out, ((1,), (0,)))

        @pl.when(c == 3)
        def _():
            dv_stage[...] = dv_acc[...].astype(BF).reshape(NY, NZ, 64, 128)
            for n, path, rows, mid in ((n_dva, "a", low, dv_mid_a), (n_dvb, "b", high, dv_mid_b)):
                first(n, path, dv_stage.at[:, :, rows], mid)
                keep(n, path, dv_stage.at[:, :, rows], mid)

        centre = jnp.sum(grad_out.astype(F32).T * mixed[c], axis=0, keepdims=True)
        grad_probs = dot(v_land[...].reshape(2048, 128), grad_out, ((1,), (1,)))
        grad_scores = (probs[c] * (grad_probs - centre)).astype(BF)
        dk_acc[...] += dot(grad_scores, qn[c], ((1,), (0,)))

        @pl.when(c == 3)
        def _():
            part_k = jnp.zeros((1, 128), F32)
            for t in range(NY):
                unit, inverse = normalize(k_land[t].reshape(512, 128).astype(F32))
                grad_norm = dk_acc[pl.ds(512 * t, 512), :] * scale
                part_k = part_k + jnp.sum(grad_norm * unit, axis=0, keepdims=True)
                out = restore(unit, inverse, grad_norm, gain_k[...]).astype(BF)
                dk_stage[t] = out.reshape(NZ, 64, 128)
            g_part[0, 1:2, :] = part_k
            for n, path, rows, mid in ((n_dka, "a", low, dk_mid_a), (n_dkb, "b", high, dk_mid_b)):
                first(n, path, dk_stage.at[:, :, rows], mid)
                keep(n, path, dk_stage.at[:, :, rows], mid)

        grad_norm = dot(kn[...], grad_scores, ((0,), (0,))).T * scale
        unit, inverse = normalize(q_land[c].reshape(QB, 128).astype(F32))
        out = restore(unit, inverse, grad_norm, gain_q[...]).astype(BF)
        dq_stage[c] = out.reshape(NZ, 64, 128)
        send_dq(c)
        return part_q + jnp.sum(grad_norm * unit, axis=0, keepdims=True)

    g_part[0, 0:1, :] = lax.fori_loop(0, 4, after, jnp.zeros((1, 128), F32))

    local(g_part.at[0], g_z.at[z], gsem.at[0])
    for dz in zo:
        remote(g_part.at[0], g_z.at[z], gsend.at[0], gsem.at[0], at_z(dz))

    second(n_dva, "a", dv_mid_a, v_out.at[:, :, low])
    second(n_dvb, "b", dv_mid_b, v_out.at[:, :, high])

    wait(g_z, gsem.at[0])
    g_part[1, :, :] = jnp.sum(g_z[...], axis=0)
    local(g_part.at[1], g_y.at[y], gsem.at[1])
    for dy in yo:
        remote(g_part.at[1], g_y.at[y], gsend.at[1], gsem.at[1], at_y(dy))

    second(n_dka, "a", dk_mid_a, k_out.at[:, :, low])
    second(n_dkb, "b", dk_mid_b, k_out.at[:, :, high])

    wait(g_y, gsem.at[1])
    g_part[2, :, :] = jnp.sum(g_y[...], axis=0)
    local(g_part.at[2], g_d.at[dp], gsem.at[2])
    for dd in range(1, n_dp):
        remote(g_part.at[2], g_d.at[dp], gsend.at[2], gsem.at[2], {"dp": (dp + dd) % n_dp})

    second(n_dqa, "a", dq_mid_a, q_out.at[:, :, low])
    second(n_dqb, "b", dq_mid_b, q_out.at[:, :, high])

    wait(g_d, gsem.at[2])
    sums = jnp.sum(g_d[...], axis=0)
    per_row = 128 * n_dp // 256
    row = jnp.where(dp // per_row == 0, sums[0:1], sums[1:2])
    start = (dp % per_row) * (256 // n_dp)
    g_out[...] = pltpu.roll(jnp.broadcast_to(row, (8, 128)), (128 - start) % 128, 1)

    for n, (path, src, mid, land) in enumerate(streams):
        sent(n, path, mid)
    sent(n_dqa, "a", dq_mid_a)
    sent(n_dqb, "b", dq_mid_b)
    sent(n_dva, "a", dv_mid_a)
    sent(n_dvb, "b", dv_mid_b)
    sent(n_dka, "a", dk_mid_a)
    sent(n_dkb, "b", dk_mid_b)
    wait(g_z.at[pl.ds(0, NZ - 1)], gsend.at[0])
    wait(g_y.at[pl.ds(0, NY - 1)], gsend.at[1])
    wait(g_d.at[pl.ds(0, n_dp - 1)], gsend.at[2])
    wait(q_out.at[:, :, low], sem2.at[n_dqa])
    wait(q_out.at[:, :, high], sem2.at[n_dqb])
    wait(v_out.at[:, :, low], sem2.at[n_dva])
    wait(v_out.at[:, :, high], sem2.at[n_dvb])
    wait(k_out.at[:, :, low], sem2.at[n_dka])
    wait(k_out.at[:, :, high], sem2.at[n_dkb])


def deliver(q_done, k_done, v_done, g_done, q_out, k_out, v_out, g_out, sem):
    pairs = ((q_done, q_out), (k_done, k_out), (v_done, v_out))
    copies = [
        pltpu.make_async_copy(src.at[part], dst.at[part], sem.at[n, part])
        for n, (src, dst) in enumerate(pairs)
        for part in range(NY)
    ]
    for copy in copies:
        copy.start()
    g_out[...] = g_done[0, 0 : g_out.shape[0]]
    for copy in copies:
        copy.wait()


def on_device(query_raw, key_raw, values, residuals, block_section, gain_query, gain_key):
    n_dp = lax.axis_size("dp")
    local_shape = query_raw.shape
    grid = (NY, NZ, 64, 128)
    vmem, dma = pltpu.VMEM, pltpu.SemaphoreType.DMA
    scratch = [
        vmem((NZ, NY, 64, 128), BF), vmem(grid, BF), vmem((2, 32, 32, 128), BF),
        *[vmem((3, 32, 16, 128), BF)] * 4,
        vmem(grid, BF), vmem(grid, BF), vmem(grid, BF),
        *[vmem((3, NY, NZ, 16, 128), BF)] * 4,
        vmem((2048, 128), BF), vmem((4, QB, 128), BF), vmem((QB, 128), F32),
        vmem((4, 2048, QB), F32), vmem((4, 2048, QB), BF), vmem((4, 128, QB), F32),
        vmem((2048, 128), F32), vmem((2048, 128), F32),
        vmem(grid, BF), vmem(grid, BF), vmem(grid, BF),
        *[vmem((NZ, NY, 32, 128), BF), vmem((NY, NZ, 32, 128), BF)] * 3,
        vmem((3, 8, 128), F32), vmem((NZ, 8, 128), F32), vmem((NY, 8, 128), F32), vmem((n_dp, 8, 128), F32),
        pltpu.SMEM((3,), jnp.int32), vmem((1, 128), F32), vmem((1, 128), F32),
        dma((22,)), dma((22,)), dma((22,)), dma((22,)), dma((3,)), dma((3,)), dma((3,)),
    ]
    anywhere = pl.BlockSpec(memory_space=pl.ANY)
    inside = pl.BlockSpec(memory_space=pltpu.VMEM)
    kept = pltpu.VMEM(grid, BF)
    operands = (
        block_section,
        gain_query.reshape(1, 128),
        gain_key.reshape(1, 128),
        query_raw.reshape(grid),
        key_raw.reshape(grid),
        values.reshape(grid),
        residuals.reshape((3,) + grid),
    )
    done = pl.pallas_call(
        kernel,
        out_shape=(kept, kept, kept, pltpu.VMEM((8, 128), F32)),
        in_specs=[anywhere] * 7,
        out_specs=(anywhere, anywhere, anywhere, inside),
        scratch_shapes=scratch,
        compiler_params=pltpu.CompilerParams(
            collective_id=0, has_side_effects=True, vmem_limit_bytes=56 << 20
        ),
        name="attention_backward",
    )(*[pltpu.with_memory_space_constraint(operand, pltpu.HBM) for operand in operands])
    full = jax.ShapeDtypeStruct(grid, BF)
    grad_q, grad_k, grad_v, grad_gains = pl.pallas_call(
        deliver,
        out_shape=(full, full, full, jax.ShapeDtypeStruct((256 // n_dp,), F32)),
        in_specs=[anywhere] * 3 + [inside],
        out_specs=(anywhere, anywhere, anywhere, inside),
        scratch_shapes=[dma((3, NY))],
        compiler_params=pltpu.CompilerParams(vmem_limit_bytes=1 << 20),
        name="deliver",
    )(*done)
    return (
        grad_q.reshape(local_shape),
        grad_k.reshape(local_shape),
        grad_v.reshape(local_shape),
        grad_gains,
    )


def solution(mesh):
    placed = (
        P("dp", None, "seq", None),
        P("dp", None, "seq", None),
        P("dp", None, "seq", None),
        P(None, "dp", None, "seq", None),
        P(),
        P(),
        P(),
    )
    return jax.shard_map(
        on_device,
        mesh=mesh,
        in_specs=placed,
        out_specs=(
            P("dp", None, "seq", None),
            P("dp", None, "seq", None),
            P("dp", None, "seq", None),
            P("dp"),
        ),
        check_vma=False,
    )
```

```python
import math

import jax
import jax.numpy as jnp
from jax import lax
from jax.experimental import pallas as pl
from jax.experimental.pallas import tpu as pltpu
from jax.sharding import PartitionSpec as P

MESH = pl.DeviceIdType.MESH
epsilon = 1e-06
NY, NZ = 4, 8
QB = 512
BF, F32 = jnp.bfloat16, jnp.float32


def dot(a, b, dims):
    return lax.dot_general(a, b, (dims, ((), ())), preferred_element_type=F32)


def normalize(entries):
    inverse = lax.rsqrt(jnp.mean(entries * entries, axis=-1, keepdims=True) + epsilon)
    return entries * inverse, inverse


def restore(unit, inverse, grad_norm, gain):
    grad_unit = grad_norm * gain
    return inverse * (grad_unit - unit * jnp.mean(grad_unit * unit, axis=-1, keepdims=True))


def kernel(
    sec_in, gain_q_in, gain_k_in, q_in, k_in, v_in, r_in,
    q_out, k_out, v_out, g_out,
    k_mid, v_mid, q_mid, r_mid0, r_mid1, r_mid2, r_mid3,
    k_land, v_land, q_land, r_land0, r_land1, r_land2, r_land3,
    kn, qn, do_f, probs, probs_b, mixed, dk_acc, dv_acc,
    dq_stage, dk_stage, dv_stage, dq_mid_a, dq_mid_b, dk_mid_a, dk_mid_b, dv_mid_a, dv_mid_b,
    g_part, g_z, g_y, g_d, sec, gain_q, gain_k,
    sem1, sem2, send1, send2, gsem, gsend, own,
):
    me = lax.axis_index("seq")
    dp = lax.axis_index("dp")
    y, z = me // NZ, me % NZ
    scale = 128 ** (-0.5)
    r_mid = (r_mid0, r_mid1, r_mid2, r_mid3)
    r_land = (r_land0, r_land1, r_land2, r_land3)
    n_dp = g_d.shape[0]

    def at_z(dz):
        return {"seq": y * NZ + (z + dz) % NZ}

    def at_y(dy):
        return {"seq": ((y + dy) % NY) * NZ + z}

    barrier = pltpu.get_barrier_semaphore()
    for dz in range(1, NZ):
        pl.semaphore_signal(barrier, 1, device_id=at_z(dz), device_id_type=MESH)
    for dy in range(1, NY):
        pl.semaphore_signal(barrier, 1, device_id=at_y(dy), device_id_type=MESH)
    for dd in range(1, n_dp):
        pl.semaphore_signal(barrier, 1, device_id={"dp": (dp + dd) % n_dp}, device_id_type=MESH)
    def local(src, dst, sem):
        pltpu.make_async_copy(src, dst, sem).start()

    def remote(src, dst, send, recv, device):
        pltpu.make_async_remote_copy(
            src_ref=src, dst_ref=dst, send_sem=send, recv_sem=recv, device_id=device, device_id_type=MESH
        ).start()

    def wait(ref, sem):
        pltpu.make_async_copy(ref, ref, sem).wait()

    zo = (4, 3, 5, 2, 6, 1, 7)
    yo = (2, 1, 3)

    def keep(n, path, src, mid):
        if path == "a":
            local(src.at[:, z], mid.at[z], sem1.at[n])
        else:
            local(src.at[y], mid.at[y], sem1.at[n])

    def first(n, path, src, mid):
        if path == "a":
            for dz in zo:
                remote(src.at[:, (z + dz) % NZ], mid.at[z], send1.at[n], sem1.at[n], at_z(dz))
        else:
            for dy in yo:
                remote(src.at[(y + dy) % NY], mid.at[y], send1.at[n], sem1.at[n], at_y(dy))

    def second(n, path, mid, land):
        wait(mid, sem1.at[n])
        if path == "a":
            local(mid.at[:, y], land.at[y], sem2.at[n])
            for dy in yo:
                remote(mid.at[:, (y + dy) % NY], land.at[y], send2.at[n], sem2.at[n], at_y(dy))
        else:
            local(mid.at[:, z], land.at[:, z], sem2.at[n])
            for dz in zo:
                remote(mid.at[:, (z + dz) % NZ], land.at[:, z], send2.at[n], sem2.at[n], at_z(dz))

    def sent(n, path, mid):
        if path == "a":
            wait(mid.at[pl.ds(0, NZ - 1)], send1.at[n])
            wait(mid.at[:, pl.ds(0, NY - 1)], send2.at[n])
        else:
            wait(mid.at[pl.ds(0, NY - 1)], send1.at[n])
            wait(mid.at[:, pl.ds(0, NZ - 1)], send2.at[n])

    low, high = pl.ds(0, 32), pl.ds(32, 32)
    streams = []
    groups = []
    for half, rows in enumerate((low, high)):
        streams.append(("b", v_in.at[:, :, rows], v_mid.at[half], v_land.at[:, :, rows]))
        streams.append(("a", k_in.at[:, :, rows], k_mid.at[half], k_land.at[:, :, rows]))
        groups.append((2 * half, 2 * half + 1))
    streams.append(("b", q_in.at[:, :, high], q_mid.at[1].reshape(NY, NZ, 32, 128), q_land.at[:, :, high]))
    streams.append(("a", q_in.at[:, :, low], q_mid.at[0].reshape(NZ, NY, 32, 128), q_land.at[:, :, low]))
    groups.append((4, 5))
    for c in range(4):
        groups.append(tuple(len(streams) + i for i in range(3)))
        for i in range(3):
            path = ("a", "b", "ab"[c % 2])[i]
            shape = (NZ, NY, 16, 128) if path == "a" else (NY, NZ, 16, 128)
            streams.append(
                (path, r_in.at[i, :, :, pl.ds(16 * c, 16)], r_mid[c].at[i].reshape(*shape), r_land[c].at[i])
            )
    n_in = len(streams)

    def first_legs(group):
        for n in groups[group]:
            path, src, mid, _ = streams[n]
            first(n, path, src, mid)

    def second_legs(group):
        for n in groups[group]:
            path, _, mid, land = streams[n]
            second(n, path, mid, land)

    def landed(group):
        for n in groups[group]:
            wait(streams[n][3], sem2.at[n])

    def own_blocks(group):
        for n in groups[group]:
            path, src, mid, _ = streams[n]
            keep(n, path, src, mid)

    for group in range(3):
        own_blocks(group)
    pl.semaphore_wait(barrier, NZ - 1 + NY - 1 + n_dp - 1)
    for group in range(5):
        first_legs(group)
    for group in range(3, 7):
        own_blocks(group)
    small = ((sec_in, sec), (gain_q_in, gain_q), (gain_k_in, gain_k))
    for n, (src, dst) in enumerate(small):
        local(src, dst, own.at[n])
    g_part[...] = jnp.zeros_like(g_part)
    dk_acc[...] = jnp.zeros_like(dk_acc)
    dv_acc[...] = jnp.zeros_like(dv_acc)
    for n, (src, dst) in enumerate(small):
        pltpu.make_async_copy(src, dst, own.at[n]).wait()
    second_legs(0)
    first_legs(5)
    second_legs(1)
    first_legs(6)
    second_legs(2)

    landed(0)
    landed(1)
    for t in range(NY):
        unit, _ = normalize(k_land[t].reshape(512, 128).astype(F32))
        kn[pl.ds(512 * t, 512), :] = (unit * gain_k[...]).astype(BF)
    second_legs(3)
    second_legs(4)
    landed(2)

    def before(c, carry):
        unit, _ = normalize(q_land[c].reshape(QB, 128).astype(F32))
        norm = (unit * gain_q[...]).astype(BF)
        qn[c] = norm
        weights = jnp.exp2(dot(kn[...], norm, ((1,), (1,))) * (scale * math.log2(math.e)))
        probs[c] = weights
        over = 1.0 / jnp.sum(weights, axis=0, keepdims=True)
        share = probs[c] * over
        upper = share.astype(BF)
        lower = (share - upper.astype(F32)).astype(BF)
        probs[c] = share
        probs_b[c] = upper
        held = v_land[...].reshape(2048, 128)
        mixed[c] = dot(held, upper, ((0,), (0,))) + dot(held, lower, ((0,), (0,)))
        return carry

    lax.fori_loop(0, 2, before, 0)
    second_legs(5)
    lax.fori_loop(2, 4, before, 0)
    second_legs(6)

    n_dqa, n_dqb, n_dva, n_dvb, n_dka, n_dkb = range(n_in, n_in + 6)

    def send_dq(c):
        local(dq_stage.at[c, z, low], dq_mid_a.at[z, c], sem1.at[n_dqa])
        for dz in zo:
            remote(
                dq_stage.at[c, (z + dz) % NZ, low], dq_mid_a.at[z, c],
                send1.at[n_dqa], sem1.at[n_dqa], at_z(dz),
            )

        @pl.when(y == c)
        def _():
            local(dq_stage.at[c, :, high], dq_mid_b.at[y], sem1.at[n_dqb])

        @pl.when(y != c)
        def _():
            remote(
                dq_stage.at[c, :, high], dq_mid_b.at[y],
                send1.at[n_dqb], sem1.at[n_dqb], {"seq": c * NZ + z},
            )

    def after(c, part_q):
        for cc in range(4):

            @pl.when(c == cc)
            def _():
                landed(3 + cc)
                for r in range(32):
                    total = None
                    for i in range(3):
                        d = (r + 32 - sec[i]) % 32
                        row = r_land[cc][i, d // NZ, d % NZ].astype(F32)
                        total = row if total is None else total + row
                    do_f[pl.ds(r, 16, stride=32), :] = total

        grad_out = do_f[...].astype(BF)
        dv_acc[...] += dot(probs_b[c], grad_out, ((1,), (0,)))

        @pl.when(c == 3)
        def _():
            dv_stage[...] = dv_acc[...].astype(BF).reshape(NY, NZ, 64, 128)
            for n, path, rows, mid in ((n_dva, "a", low, dv_mid_a), (n_dvb, "b", high, dv_mid_b)):
                first(n, path, dv_stage.at[:, :, rows], mid)
                keep(n, path, dv_stage.at[:, :, rows], mid)

        centre = jnp.sum(grad_out.astype(F32).T * mixed[c], axis=0, keepdims=True)
        grad_probs = dot(v_land[...].reshape(2048, 128), grad_out, ((1,), (1,)))
        grad_scores = (probs[c] * (grad_probs - centre)).astype(BF)
        dk_acc[...] += dot(grad_scores, qn[c], ((1,), (0,)))

        @pl.when(c == 3)
        def _():
            part_k = jnp.zeros((1, 128), F32)
            for t in range(NY):
                unit, inverse = normalize(k_land[t].reshape(512, 128).astype(F32))
                grad_norm = dk_acc[pl.ds(512 * t, 512), :] * scale
                part_k = part_k + jnp.sum(grad_norm * unit, axis=0, keepdims=True)
                out = restore(unit, inverse, grad_norm, gain_k[...]).astype(BF)
                dk_stage[t] = out.reshape(NZ, 64, 128)
            g_part[0, 1:2, :] = part_k
            for n, path, rows, mid in ((n_dka, "a", low, dk_mid_a), (n_dkb, "b", high, dk_mid_b)):
                first(n, path, dk_stage.at[:, :, rows], mid)
                keep(n, path, dk_stage.at[:, :, rows], mid)

        grad_norm = dot(kn[...], grad_scores, ((0,), (0,))).T * scale
        unit, inverse = normalize(q_land[c].reshape(QB, 128).astype(F32))
        out = restore(unit, inverse, grad_norm, gain_q[...]).astype(BF)
        dq_stage[c] = out.reshape(NZ, 64, 128)
        send_dq(c)
        return part_q + jnp.sum(grad_norm * unit, axis=0, keepdims=True)

    g_part[0, 0:1, :] = lax.fori_loop(0, 4, after, jnp.zeros((1, 128), F32))

    local(g_part.at[0], g_z.at[z], gsem.at[0])
    for dz in zo:
        remote(g_part.at[0], g_z.at[z], gsend.at[0], gsem.at[0], at_z(dz))

    second(n_dva, "a", dv_mid_a, v_out.at[:, :, low])
    second(n_dvb, "b", dv_mid_b, v_out.at[:, :, high])

    wait(g_z, gsem.at[0])
    g_part[1, :, :] = jnp.sum(g_z[...], axis=0)
    local(g_part.at[1], g_y.at[y], gsem.at[1])
    for dy in yo:
        remote(g_part.at[1], g_y.at[y], gsend.at[1], gsem.at[1], at_y(dy))

    second(n_dka, "a", dk_mid_a, k_out.at[:, :, low])
    second(n_dkb, "b", dk_mid_b, k_out.at[:, :, high])

    second(n_dqa, "a", dq_mid_a, q_out.at[:, :, low])
    second(n_dqb, "b", dq_mid_b, q_out.at[:, :, high])

    wait(g_y, gsem.at[1])
    g_part[2, :, :] = jnp.sum(g_y[...], axis=0)
    local(g_part.at[2], g_d.at[dp], gsem.at[2])
    for dd in range(1, n_dp):
        remote(g_part.at[2], g_d.at[dp], gsend.at[2], gsem.at[2], {"dp": (dp + dd) % n_dp})

    wait(g_d, gsem.at[2])
    sums = jnp.sum(g_d[...], axis=0)
    per_row = 128 * n_dp // 256
    row = jnp.where(dp // per_row == 0, sums[0:1], sums[1:2])
    start = (dp % per_row) * (256 // n_dp)
    g_out[...] = pltpu.roll(jnp.broadcast_to(row, (8, 128)), (128 - start) % 128, 1)

    for n, (path, src, mid, land) in enumerate(streams):
        sent(n, path, mid)
    sent(n_dqa, "a", dq_mid_a)
    sent(n_dqb, "b", dq_mid_b)
    sent(n_dva, "a", dv_mid_a)
    sent(n_dvb, "b", dv_mid_b)
    sent(n_dka, "a", dk_mid_a)
    sent(n_dkb, "b", dk_mid_b)
    wait(g_z.at[pl.ds(0, NZ - 1)], gsend.at[0])
    wait(g_y.at[pl.ds(0, NY - 1)], gsend.at[1])
    wait(g_d.at[pl.ds(0, n_dp - 1)], gsend.at[2])
    wait(q_out.at[:, :, low], sem2.at[n_dqa])
    wait(q_out.at[:, :, high], sem2.at[n_dqb])
    wait(v_out.at[:, :, low], sem2.at[n_dva])
    wait(v_out.at[:, :, high], sem2.at[n_dvb])
    wait(k_out.at[:, :, low], sem2.at[n_dka])
    wait(k_out.at[:, :, high], sem2.at[n_dkb])


def deliver(q_done, k_done, v_done, g_done, q_out, k_out, v_out, g_out, sem):
    pairs = ((q_done, q_out), (k_done, k_out), (v_done, v_out))
    copies = [
        pltpu.make_async_copy(src.at[part], dst.at[part], sem.at[n, part])
        for n, (src, dst) in enumerate(pairs)
        for part in range(NY)
    ]
    for copy in copies:
        copy.start()
    g_out[...] = g_done[0, 0 : g_out.shape[0]]
    for copy in copies:
        copy.wait()


def on_device(query_raw, key_raw, values, residuals, block_section, gain_query, gain_key):
    n_dp = lax.axis_size("dp")
    local_shape = query_raw.shape
    grid = (NY, NZ, 64, 128)
    vmem, dma = pltpu.VMEM, pltpu.SemaphoreType.DMA
    scratch = [
        vmem((2, NZ, NY, 32, 128), BF), vmem((2, NY, NZ, 32, 128), BF), vmem((2, 32, 32, 128), BF),
        *[vmem((3, 32, 16, 128), BF)] * 4,
        vmem(grid, BF), vmem(grid, BF), vmem(grid, BF),
        *[vmem((3, NY, NZ, 16, 128), BF)] * 4,
        vmem((2048, 128), BF), vmem((4, QB, 128), BF), vmem((QB, 128), F32),
        vmem((4, 2048, QB), F32), vmem((4, 2048, QB), BF), vmem((4, 128, QB), F32),
        vmem((2048, 128), F32), vmem((2048, 128), F32),
        vmem(grid, BF), vmem(grid, BF), vmem(grid, BF),
        *[vmem((NZ, NY, 32, 128), BF), vmem((NY, NZ, 32, 128), BF)] * 3,
        vmem((3, 8, 128), F32), vmem((NZ, 8, 128), F32), vmem((NY, 8, 128), F32), vmem((n_dp, 8, 128), F32),
        pltpu.SMEM((3,), jnp.int32), vmem((1, 128), F32), vmem((1, 128), F32),
        dma((24,)), dma((24,)), dma((24,)), dma((24,)), dma((3,)), dma((3,)), dma((3,)),
    ]
    anywhere = pl.BlockSpec(memory_space=pl.ANY)
    inside = pl.BlockSpec(memory_space=pltpu.VMEM)
    kept = pltpu.VMEM(grid, BF)
    operands = (
        block_section,
        gain_query.reshape(1, 128),
        gain_key.reshape(1, 128),
        query_raw.reshape(grid),
        key_raw.reshape(grid),
        values.reshape(grid),
        residuals.reshape((3,) + grid),
    )
    done = pl.pallas_call(
        kernel,
        out_shape=(kept, kept, kept, pltpu.VMEM((8, 128), F32)),
        in_specs=[anywhere] * 7,
        out_specs=(anywhere, anywhere, anywhere, inside),
        scratch_shapes=scratch,
        compiler_params=pltpu.CompilerParams(
            collective_id=0, has_side_effects=True, vmem_limit_bytes=56 << 20
        ),
        name="attention_backward",
    )(*[pltpu.with_memory_space_constraint(operand, pltpu.HBM) for operand in operands])
    full = jax.ShapeDtypeStruct(grid, BF)
    grad_q, grad_k, grad_v, grad_gains = pl.pallas_call(
        deliver,
        out_shape=(full, full, full, jax.ShapeDtypeStruct((256 // n_dp,), F32)),
        in_specs=[anywhere] * 3 + [inside],
        out_specs=(anywhere, anywhere, anywhere, inside),
        scratch_shapes=[dma((3, NY))],
        compiler_params=pltpu.CompilerParams(vmem_limit_bytes=1 << 20),
        name="deliver",
    )(*done)
    return (
        grad_q.reshape(local_shape),
        grad_k.reshape(local_shape),
        grad_v.reshape(local_shape),
        grad_gains,
    )


def solution(mesh):
    placed = (
        P("dp", None, "seq", None),
        P("dp", None, "seq", None),
        P("dp", None, "seq", None),
        P(None, "dp", None, "seq", None),
        P(),
        P(),
        P(),
    )
    return jax.shard_map(
        on_device,
        mesh=mesh,
        in_specs=placed,
        out_specs=(
            P("dp", None, "seq", None),
            P("dp", None, "seq", None),
            P("dp", None, "seq", None),
            P("dp"),
        ),
        check_vma=False,
    )
```

```python
import math

import jax
import jax.numpy as jnp
from jax import lax
from jax.experimental import pallas as pl
from jax.experimental.pallas import tpu as pltpu
from jax.sharding import PartitionSpec as P

MESH = pl.DeviceIdType.MESH
epsilon = 1e-06
NY, NZ = 4, 8
QB = 512
BF, F32 = jnp.bfloat16, jnp.float32


def dot(a, b, dims):
    return lax.dot_general(a, b, (dims, ((), ())), preferred_element_type=F32)


def normalize(entries):
    inverse = lax.rsqrt(jnp.mean(entries * entries, axis=-1, keepdims=True) + epsilon)
    return entries * inverse, inverse


def restore(unit, inverse, grad_norm, gain):
    grad_unit = grad_norm * gain
    return inverse * (grad_unit - unit * jnp.mean(grad_unit * unit, axis=-1, keepdims=True))


def kernel(
    sec_in, gain_q_in, gain_k_in, q_in, k_in, v_in, r_in,
    q_out, k_out, v_out, g_out,
    k_mid, v_mid, q_mid, r_mid0, r_mid1, r_mid2, r_mid3,
    k_land, v_land, q_land, r_land0, r_land1, r_land2, r_land3,
    kn, qn, do_f, probs, probs_b, mixed, dk_acc, dv_acc,
    dq_stage, dk_stage, dv_stage, dq_mid_a, dq_mid_b, dk_mid_a, dk_mid_b, dv_mid_a, dv_mid_b,
    g_part, g_z, g_y, g_d, sec, gain_q, gain_k,
    sem1, sem2, send1, send2, gsem, gsend, own,
):
    me = lax.axis_index("seq")
    dp = lax.axis_index("dp")
    y, z = me // NZ, me % NZ
    scale = 128 ** (-0.5)
    r_mid = (r_mid0, r_mid1, r_mid2, r_mid3)
    r_land = (r_land0, r_land1, r_land2, r_land3)
    n_dp = g_d.shape[0]

    def at_z(dz):
        return {"seq": y * NZ + (z + dz) % NZ}

    def at_y(dy):
        return {"seq": ((y + dy) % NY) * NZ + z}

    barrier = pltpu.get_barrier_semaphore()
    for dz in range(1, NZ):
        pl.semaphore_signal(barrier, 1, device_id=at_z(dz), device_id_type=MESH)
    for dy in range(1, NY):
        pl.semaphore_signal(barrier, 1, device_id=at_y(dy), device_id_type=MESH)
    for dd in range(1, n_dp):
        pl.semaphore_signal(barrier, 1, device_id={"dp": (dp + dd) % n_dp}, device_id_type=MESH)
    def local(src, dst, sem):
        pltpu.make_async_copy(src, dst, sem).start()

    def remote(src, dst, send, recv, device):
        pltpu.make_async_remote_copy(
            src_ref=src, dst_ref=dst, send_sem=send, recv_sem=recv, device_id=device, device_id_type=MESH
        ).start()

    def wait(ref, sem):
        pltpu.make_async_copy(ref, ref, sem).wait()

    zo = (4, 3, 5, 2, 6, 1, 7)
    yo = (2, 1, 3)

    def keep(n, path, src, mid):
        if path == "a":
            local(src.at[:, z], mid.at[z], sem1.at[n])
        else:
            local(src.at[y], mid.at[y], sem1.at[n])

    def first(n, path, src, mid):
        if path == "a":
            for dz in zo:
                remote(src.at[:, (z + dz) % NZ], mid.at[z], send1.at[n], sem1.at[n], at_z(dz))
        else:
            for dy in yo:
                remote(src.at[(y + dy) % NY], mid.at[y], send1.at[n], sem1.at[n], at_y(dy))

    def second(n, path, mid, land):
        wait(mid, sem1.at[n])
        if path == "a":
            local(mid.at[:, y], land.at[y], sem2.at[n])
            for dy in yo:
                remote(mid.at[:, (y + dy) % NY], land.at[y], send2.at[n], sem2.at[n], at_y(dy))
        else:
            local(mid.at[:, z], land.at[:, z], sem2.at[n])
            for dz in zo:
                remote(mid.at[:, (z + dz) % NZ], land.at[:, z], send2.at[n], sem2.at[n], at_z(dz))

    def sent(n, path, mid):
        if path == "a":
            wait(mid.at[pl.ds(0, NZ - 1)], send1.at[n])
            wait(mid.at[:, pl.ds(0, NY - 1)], send2.at[n])
        else:
            wait(mid.at[pl.ds(0, NY - 1)], send1.at[n])
            wait(mid.at[:, pl.ds(0, NZ - 1)], send2.at[n])

    low, high = pl.ds(0, 32), pl.ds(32, 32)
    streams = []
    groups = []
    for half, rows in enumerate((low, high)):
        streams.append(("b", v_in.at[:, :, rows], v_mid.at[half], v_land.at[:, :, rows]))
        streams.append(("a", k_in.at[:, :, rows], k_mid.at[half], k_land.at[:, :, rows]))
        groups.append((2 * half, 2 * half + 1))
    streams.append(("b", q_in.at[:, :, high], q_mid.at[1].reshape(NY, NZ, 32, 128), q_land.at[:, :, high]))
    streams.append(("a", q_in.at[:, :, low], q_mid.at[0].reshape(NZ, NY, 32, 128), q_land.at[:, :, low]))
    groups.append((4, 5))
    for c in range(4):
        groups.append(tuple(len(streams) + i for i in range(3)))
        for i in range(3):
            path = ("a", "b", "ab"[c % 2])[i]
            shape = (NZ, NY, 16, 128) if path == "a" else (NY, NZ, 16, 128)
            streams.append(
                (path, r_in.at[i, :, :, pl.ds(16 * c, 16)], r_mid[c].at[i].reshape(*shape), r_land[c].at[i])
            )
    n_in = len(streams)

    def first_legs(group):
        for n in groups[group]:
            path, src, mid, _ = streams[n]
            first(n, path, src, mid)

    def second_legs(group):
        for n in groups[group]:
            path, _, mid, land = streams[n]
            second(n, path, mid, land)

    def landed(group):
        for n in groups[group]:
            wait(streams[n][3], sem2.at[n])

    def own_blocks(group):
        for n in groups[group]:
            path, src, mid, _ = streams[n]
            keep(n, path, src, mid)

    for group in range(3):
        own_blocks(group)
    pl.semaphore_wait(barrier, NZ - 1 + NY - 1 + n_dp - 1)
    for group in range(5):
        first_legs(group)
    for group in range(3, 7):
        own_blocks(group)
    small = ((sec_in, sec), (gain_q_in, gain_q), (gain_k_in, gain_k))
    for n, (src, dst) in enumerate(small):
        local(src, dst, own.at[n])
    g_part[...] = jnp.zeros_like(g_part)
    dk_acc[...] = jnp.zeros_like(dk_acc)
    dv_acc[...] = jnp.zeros_like(dv_acc)
    for n, (src, dst) in enumerate(small):
        pltpu.make_async_copy(src, dst, own.at[n]).wait()
    second_legs(0)
    first_legs(5)
    second_legs(1)
    first_legs(6)
    second_legs(2)

    landed(0)
    landed(1)
    for t in range(NY):
        unit, _ = normalize(k_land[t].reshape(512, 128).astype(F32))
        kn[pl.ds(512 * t, 512), :] = (unit * gain_k[...]).astype(BF)
    second_legs(3)
    second_legs(4)
    landed(2)

    def before(c, carry):
        unit, _ = normalize(q_land[c].reshape(QB, 128).astype(F32))
        norm = (unit * gain_q[...]).astype(BF)
        qn[c] = norm
        weights = jnp.exp2(dot(kn[...], norm, ((1,), (1,))) * (scale * math.log2(math.e)))
        probs[c] = weights
        over = 1.0 / jnp.sum(weights, axis=0, keepdims=True)
        share = probs[c] * over
        upper = share.astype(BF)
        lower = (share - upper.astype(F32)).astype(BF)
        probs[c] = share
        probs_b[c] = upper
        held = v_land[...].reshape(2048, 128)
        mixed[c] = dot(held, upper, ((0,), (0,))) + dot(held, lower, ((0,), (0,)))
        return carry

    lax.fori_loop(0, 1, before, 0)
    second_legs(5)
    lax.fori_loop(1, 4, before, 0)
    second_legs(6)

    n_dqa, n_dqb, n_dva, n_dvb, n_dka, n_dkb = range(n_in, n_in + 6)

    def send_dq(c):
        local(dq_stage.at[c, z, low], dq_mid_a.at[z, c], sem1.at[n_dqa])
        for dz in zo:
            remote(
                dq_stage.at[c, (z + dz) % NZ, low], dq_mid_a.at[z, c],
                send1.at[n_dqa], sem1.at[n_dqa], at_z(dz),
            )

        @pl.when(y == c)
        def _():
            local(dq_stage.at[c, :, high], dq_mid_b.at[y], sem1.at[n_dqb])

        @pl.when(y != c)
        def _():
            remote(
                dq_stage.at[c, :, high], dq_mid_b.at[y],
                send1.at[n_dqb], sem1.at[n_dqb], {"seq": c * NZ + z},
            )

    def after(c, part_q):
        for cc in range(4):

            @pl.when(c == cc)
            def _():
                landed(3 + cc)
                for r in range(32):
                    total = None
                    for i in range(3):
                        d = (r + 32 - sec[i]) % 32
                        row = r_land[cc][i, d // NZ, d % NZ].astype(F32)
                        total = row if total is None else total + row
                    do_f[pl.ds(r, 16, stride=32), :] = total

        grad_out = do_f[...].astype(BF)
        dv_acc[...] += dot(probs_b[c], grad_out, ((1,), (0,)))

        @pl.when(c == 3)
        def _():
            dv_stage[...] = dv_acc[...].astype(BF).reshape(NY, NZ, 64, 128)
            for n, path, rows, mid in ((n_dva, "a", low, dv_mid_a), (n_dvb, "b", high, dv_mid_b)):
                first(n, path, dv_stage.at[:, :, rows], mid)
                keep(n, path, dv_stage.at[:, :, rows], mid)

        centre = jnp.sum(grad_out.astype(F32).T * mixed[c], axis=0, keepdims=True)
        grad_probs = dot(v_land[...].reshape(2048, 128), grad_out, ((1,), (1,)))
        grad_scores = (probs[c] * (grad_probs - centre)).astype(BF)
        dk_acc[...] += dot(grad_scores, qn[c], ((1,), (0,)))

        @pl.when(c == 3)
        def _():
            part_k = jnp.zeros((1, 128), F32)
            for t in range(NY):
                unit, inverse = normalize(k_land[t].reshape(512, 128).astype(F32))
                grad_norm = dk_acc[pl.ds(512 * t, 512), :] * scale
                part_k = part_k + jnp.sum(grad_norm * unit, axis=0, keepdims=True)
                out = restore(unit, inverse, grad_norm, gain_k[...]).astype(BF)
                dk_stage[t] = out.reshape(NZ, 64, 128)
            g_part[0, 1:2, :] = part_k
            for n, path, rows, mid in ((n_dka, "a", low, dk_mid_a), (n_dkb, "b", high, dk_mid_b)):
                first(n, path, dk_stage.at[:, :, rows], mid)
                keep(n, path, dk_stage.at[:, :, rows], mid)

        grad_norm = dot(kn[...], grad_scores, ((0,), (0,))).T * scale
        unit, inverse = normalize(q_land[c].reshape(QB, 128).astype(F32))
        out = restore(unit, inverse, grad_norm, gain_q[...]).astype(BF)
        dq_stage[c] = out.reshape(NZ, 64, 128)
        send_dq(c)
        return part_q + jnp.sum(grad_norm * unit, axis=0, keepdims=True)

    g_part[0, 0:1, :] = lax.fori_loop(0, 4, after, jnp.zeros((1, 128), F32))

    local(g_part.at[0], g_z.at[z], gsem.at[0])
    for dz in zo:
        remote(g_part.at[0], g_z.at[z], gsend.at[0], gsem.at[0], at_z(dz))

    second(n_dva, "a", dv_mid_a, v_out.at[:, :, low])
    second(n_dvb, "b", dv_mid_b, v_out.at[:, :, high])

    wait(g_z, gsem.at[0])
    g_part[1, :, :] = jnp.sum(g_z[...], axis=0)
    local(g_part.at[1], g_y.at[y], gsem.at[1])
    for dy in yo:
        remote(g_part.at[1], g_y.at[y], gsend.at[1], gsem.at[1], at_y(dy))

    second(n_dka, "a", dk_mid_a, k_out.at[:, :, low])
    second(n_dkb, "b", dk_mid_b, k_out.at[:, :, high])

    second(n_dqa, "a", dq_mid_a, q_out.at[:, :, low])
    second(n_dqb, "b", dq_mid_b, q_out.at[:, :, high])

    wait(g_y, gsem.at[1])
    g_part[2, :, :] = jnp.sum(g_y[...], axis=0)
    local(g_part.at[2], g_d.at[dp], gsem.at[2])
    for dd in range(1, n_dp):
        remote(g_part.at[2], g_d.at[dp], gsend.at[2], gsem.at[2], {"dp": (dp + dd) % n_dp})

    wait(g_d, gsem.at[2])
    sums = jnp.sum(g_d[...], axis=0)
    per_row = 128 * n_dp // 256
    row = jnp.where(dp // per_row == 0, sums[0:1], sums[1:2])
    start = (dp % per_row) * (256 // n_dp)
    g_out[...] = pltpu.roll(jnp.broadcast_to(row, (8, 128)), (128 - start) % 128, 1)

    for n, (path, src, mid, land) in enumerate(streams):
        sent(n, path, mid)
    sent(n_dqa, "a", dq_mid_a)
    sent(n_dqb, "b", dq_mid_b)
    sent(n_dva, "a", dv_mid_a)
    sent(n_dvb, "b", dv_mid_b)
    sent(n_dka, "a", dk_mid_a)
    sent(n_dkb, "b", dk_mid_b)
    wait(g_z.at[pl.ds(0, NZ - 1)], gsend.at[0])
    wait(g_y.at[pl.ds(0, NY - 1)], gsend.at[1])
    wait(g_d.at[pl.ds(0, n_dp - 1)], gsend.at[2])
    wait(q_out.at[:, :, low], sem2.at[n_dqa])
    wait(q_out.at[:, :, high], sem2.at[n_dqb])
    wait(v_out.at[:, :, low], sem2.at[n_dva])
    wait(v_out.at[:, :, high], sem2.at[n_dvb])
    wait(k_out.at[:, :, low], sem2.at[n_dka])
    wait(k_out.at[:, :, high], sem2.at[n_dkb])


def deliver(q_done, k_done, v_done, g_done, q_out, k_out, v_out, g_out, sem):
    pairs = ((q_done, q_out), (k_done, k_out), (v_done, v_out))
    copies = [
        pltpu.make_async_copy(src.at[part], dst.at[part], sem.at[n, part])
        for n, (src, dst) in enumerate(pairs)
        for part in range(NY)
    ]
    for copy in copies:
        copy.start()
    g_out[...] = g_done[0, 0 : g_out.shape[0]]
    for copy in copies:
        copy.wait()


def on_device(query_raw, key_raw, values, residuals, block_section, gain_query, gain_key):
    n_dp = lax.axis_size("dp")
    local_shape = query_raw.shape
    grid = (NY, NZ, 64, 128)
    vmem, dma = pltpu.VMEM, pltpu.SemaphoreType.DMA
    scratch = [
        vmem((2, NZ, NY, 32, 128), BF), vmem((2, NY, NZ, 32, 128), BF), vmem((2, 32, 32, 128), BF),
        *[vmem((3, 32, 16, 128), BF)] * 4,
        vmem(grid, BF), vmem(grid, BF), vmem(grid, BF),
        *[vmem((3, NY, NZ, 16, 128), BF)] * 4,
        vmem((2048, 128), BF), vmem((4, QB, 128), BF), vmem((QB, 128), F32),
        vmem((4, 2048, QB), F32), vmem((4, 2048, QB), BF), vmem((4, 128, QB), F32),
        vmem((2048, 128), F32), vmem((2048, 128), F32),
        vmem(grid, BF), vmem(grid, BF), vmem(grid, BF),
        *[vmem((NZ, NY, 32, 128), BF), vmem((NY, NZ, 32, 128), BF)] * 3,
        vmem((3, 8, 128), F32), vmem((NZ, 8, 128), F32), vmem((NY, 8, 128), F32), vmem((n_dp, 8, 128), F32),
        pltpu.SMEM((3,), jnp.int32), vmem((1, 128), F32), vmem((1, 128), F32),
        dma((24,)), dma((24,)), dma((24,)), dma((24,)), dma((3,)), dma((3,)), dma((3,)),
    ]
    anywhere = pl.BlockSpec(memory_space=pl.ANY)
    inside = pl.BlockSpec(memory_space=pltpu.VMEM)
    kept = pltpu.VMEM(grid, BF)
    operands = (
        block_section,
        gain_query.reshape(1, 128),
        gain_key.reshape(1, 128),
        query_raw.reshape(grid),
        key_raw.reshape(grid),
        values.reshape(grid),
        residuals.reshape((3,) + grid),
    )
    done = pl.pallas_call(
        kernel,
        out_shape=(kept, kept, kept, pltpu.VMEM((8, 128), F32)),
        in_specs=[anywhere] * 7,
        out_specs=(anywhere, anywhere, anywhere, inside),
        scratch_shapes=scratch,
        compiler_params=pltpu.CompilerParams(
            collective_id=0, has_side_effects=True, vmem_limit_bytes=56 << 20
        ),
        name="attention_backward",
    )(*[pltpu.with_memory_space_constraint(operand, pltpu.HBM) for operand in operands])
    full = jax.ShapeDtypeStruct(grid, BF)
    grad_q, grad_k, grad_v, grad_gains = pl.pallas_call(
        deliver,
        out_shape=(full, full, full, jax.ShapeDtypeStruct((256 // n_dp,), F32)),
        in_specs=[anywhere] * 3 + [inside],
        out_specs=(anywhere, anywhere, anywhere, inside),
        scratch_shapes=[dma((3, NY))],
        compiler_params=pltpu.CompilerParams(vmem_limit_bytes=1 << 20),
        name="deliver",
    )(*done)
    return (
        grad_q.reshape(local_shape),
        grad_k.reshape(local_shape),
        grad_v.reshape(local_shape),
        grad_gains,
    )


def solution(mesh):
    placed = (
        P("dp", None, "seq", None),
        P("dp", None, "seq", None),
        P("dp", None, "seq", None),
        P(None, "dp", None, "seq", None),
        P(),
        P(),
        P(),
    )
    return jax.shard_map(
        on_device,
        mesh=mesh,
        in_specs=placed,
        out_specs=(
            P("dp", None, "seq", None),
            P("dp", None, "seq", None),
            P("dp", None, "seq", None),
            P("dp"),
        ),
        check_vma=False,
    )
```
